32 devices in a mesh: leaf: 32 (over z, y, x, core).
Axes of the slice: x: 2, y: 2, z: 4, core: 2. Of those that a mesh axis runs over, the one named last changes fastest.
Arguments:
- values: bfloat16 [8192, 8, 128], P('leaf'), may hold values from -6 to 6
- points: bfloat16 [8192, 2, 128], P('leaf'), may hold values from 0 to 6
- basis: bfloat16 [8192, 64, 128], P('leaf'), may hold values from -0.5 to 0.5
- leaf_up: bfloat16 [8192, 4096], P('leaf'), may hold values from -0.5 to 0.5
- mid_up: bfloat16 [2048, 4096], P('leaf'), may hold values from -0.5 to 0.5
- box_up: bfloat16 [512, 4096], P('leaf'), may hold values from -0.5 to 0.5
- leaf_skel: bfloat16 [8192, 128], P('leaf'), may hold values from 0 to 6
- mid_skel: bfloat16 [2048, 128], P('leaf'), may hold values from 0 to 6
- box_skel: bfloat16 [512, 128], P('leaf'), may hold values from 0 to 6
- top_skel: bfloat16 [128, 128], replicated, may hold values from 0 to 6
- near_src: int32 [8192, 9], P('leaf'), may hold values from 0 to 8191, as said below
- near_count: int32 [8192], P('leaf'), may hold values from 1 to 9
- leaf_src: int32 [8192, 27], P('leaf'), may hold values from 0 to 8191, as said below
- leaf_count: int32 [8192], P('leaf'), may hold values from 1 to 27
- mid_src: int32 [2048, 27], P('leaf'), may hold values from 0 to 2047, as said below
- mid_count: int32 [2048], P('leaf'), may hold values from 1 to 27
- box_src: int32 [512, 27], P('leaf'), may hold values from 0 to 511, as said below
- box_count: int32 [512], P('leaf'), may hold values from 1 to 27
- box_parent: int32 [512], replicated, may hold values from 0 to 127, as said below
- top_src: int32 [128, 27], P('leaf'), may hold values from 0 to 127
- top_count: int32 [128], P('leaf'), may hold values from 1 to 27
Outputs:
- potential: float32 [8192, 8, 128], P('leaf')
The draws below stay inside these ranges and needn't reach their ends.
Inputs may be any that keep to these rules, and one draw needn't show every extreme that they name: `near_src`: every entry of a leaf's list lies on the device of that leaf or on one of the two beside it along leaf; slots past the count hold valid indices too. `leaf_src`: every entry lies on the device of its node or on one of the two beside it along leaf. `mid_src`: every entry lies on the device of its node or on one of the two beside it along leaf. `box_src`: every entry lies on the device of its node or on one of the two beside it along leaf. `box_parent`: every top node is the parent of exactly four level-two nodes, and these are the boxes 4k .. 4k + 3 for some k, all held on one device.
All inputs are finite; a program needn't handle non-finite values.
Results may differ from the reference program's by a relative error of at most 0.0095.
Values may be sent and summed in bfloat16 or wider, within the bound.
A program may use at most 64 MiB of HBM per device.

```python
import jax
import jax.numpy as jnp
from jax import lax

P_SIZE = 128
R = 64
S = 8
KN = 9
KF = 27
LEAF_DEV = 256
LEAVES = 8192
MIDS = 2048
BOXES = 512
TOP = 128


def neighbour_lists(key, nodes, per_device, slots):
    row_ids = jnp.arange(nodes, dtype=jnp.int32)[:, None]
    offsets = jax.random.randint(key, (nodes, slots), -per_device, per_device + 1, dtype=jnp.int32)
    return jnp.clip(row_ids + offsets, 0, nodes - 1).astype(jnp.int32)


def skewed_counts(key, nodes, per_device, most):
    devices = nodes // per_device
    first, second, third, fourth = jax.random.split(key, 4)
    divisor = jax.random.randint(first, (devices,), 1, 5, dtype=jnp.int32)
    density = jnp.maximum(most // divisor, 2)
    density = density.at[jax.random.randint(second, (), 0, devices, dtype=jnp.int32)].set(most)
    counts = jax.random.randint(third, (devices, per_device), 1, density[:, None] + 1, dtype=jnp.int32)
    position = jax.random.randint(fourth, (devices,), 0, per_device, dtype=jnp.int32)
    counts = jnp.where(jnp.arange(per_device, dtype=jnp.int32)[None, :] == position[:, None], density[:, None], counts)
    return counts.reshape(nodes).astype(jnp.int32)


def draw_near_src(key, part):
    return neighbour_lists(jax.random.fold_in(key, 101), LEAVES, LEAF_DEV, KN)


def draw_near_count(key, part):
    return skewed_counts(jax.random.fold_in(key, 102), LEAVES, LEAF_DEV, KN)


def draw_leaf_src(key, part):
    return neighbour_lists(jax.random.fold_in(key, 103), LEAVES, LEAF_DEV, KF)


def draw_leaf_count(key, part):
    return skewed_counts(jax.random.fold_in(key, 104), LEAVES, LEAF_DEV, KF)


def draw_mid_src(key, part):
    return neighbour_lists(jax.random.fold_in(key, 105), MIDS, LEAF_DEV // 4, KF)


def draw_mid_count(key, part):
    return skewed_counts(jax.random.fold_in(key, 106), MIDS, LEAF_DEV // 4, KF)


def draw_box_src(key, part):
    return neighbour_lists(jax.random.fold_in(key, 107), BOXES, LEAF_DEV // 16, KF)


def draw_box_count(key, part):
    return skewed_counts(jax.random.fold_in(key, 108), BOXES, LEAF_DEV // 16, KF)


def draw_top_count(key, part):
    return skewed_counts(jax.random.fold_in(key, 109), TOP, LEAF_DEV // 64, KF)


def draw_box_parent(key, part):
    order = jax.random.permutation(jax.random.fold_in(key, 110), TOP).astype(jnp.int32)
    return order[jnp.arange(BOXES, dtype=jnp.int32) // 4].astype(jnp.int32)


def with_ends(array, rng, least, high):
    longest = array.shape.index(max(array.shape))
    spots = []
    for shift in (0, 1):
        where = [jax.random.randint(jax.random.fold_in(rng, axis), (), 0, length) for axis, length in enumerate(array.shape)]
        where[longest] = (where[longest] + shift) % array.shape[longest]
        spots.append(tuple(where))
    return array.at[spots[0]].set(least).at[spots[1]].set(high)


def levels(own_key, extent, pieces, low, largest):
    loudness = 1.0
    for dim, shards_of in pieces:
        draws = jax.random.uniform(jax.random.fold_in(jax.random.fold_in(own_key, 6), dim), (shards_of,), jnp.float32, low / len(pieces), largest / len(pieces))
        loudness = loudness * jnp.repeat(jnp.exp(draws), extent[dim] // shards_of).reshape((-1,) + (1,) * (len(extent) - 1 - dim))
    return loudness


def gaussian(own_key, shape, deviation, limit, cuts=(), kind=jnp.bfloat16):
    array = jax.random.normal(own_key, shape, jnp.float32) * deviation
    if len(cuts) > 0:
        array = levels(own_key, shape, cuts, -0.22, 0.18) * array
    return jnp.clip(array, min=-limit, max=limit).astype(kind)


def setup_inputs(seed: int = 0) -> dict:
    splits = jax.random.split(jax.random.key(seed), 22)
    values = gaussian(splits[0], (LEAVES, S, P_SIZE), 1.0, 6.0, ((0, 32),))
    points = jnp.clip(6.0 * jax.random.uniform(splits[1], (LEAVES, 2, P_SIZE), jnp.float32) ** levels(splits[1], (LEAVES, 2, P_SIZE), ((0, 32),), -0.2, 0.2), 0.0, 6.0).astype(jnp.bfloat16)
    basis = gaussian(splits[2], (LEAVES, R, P_SIZE), P_SIZE ** -0.5, 0.5, ((0, 32),))
    leaf_up = gaussian(splits[3], (LEAVES, R * R), (2 * R) ** -0.5, 0.5, ((0, 32),))
    mid_up = gaussian(splits[4], (MIDS, R * R), (2 * R) ** -0.5, 0.5, ((0, 32),))
    box_up = gaussian(splits[5], (BOXES, R * R), (2 * R) ** -0.5, 0.5, ((0, 32),))
    leaf_skel = jnp.clip(6.0 * jax.random.uniform(splits[6], (LEAVES, 2 * R), jnp.float32) ** levels(splits[6], (LEAVES, 2 * R), ((0, 32),), -0.2, 0.2), 0.0, 6.0).astype(jnp.bfloat16)
    mid_skel = jnp.clip(6.0 * jax.random.uniform(splits[7], (MIDS, 2 * R), jnp.float32) ** levels(splits[7], (MIDS, 2 * R), ((0, 32),), -0.2, 0.2), 0.0, 6.0).astype(jnp.bfloat16)
    box_skel = jnp.clip(6.0 * jax.random.uniform(splits[8], (BOXES, 2 * R), jnp.float32) ** levels(splits[8], (BOXES, 2 * R), ((0, 32),), -0.2, 0.2), 0.0, 6.0).astype(jnp.bfloat16)
    top_skel = jnp.clip(jax.random.uniform(splits[9], (TOP, 2 * R), jnp.float32, 0.0, 6.0), 0.0, 6.0).astype(jnp.bfloat16)
    near_src = draw_near_src(jax.random.fold_in(splits[21], 71), 0)
    near_count = draw_near_count(jax.random.fold_in(splits[21], 71), 0)
    leaf_src = draw_leaf_src(jax.random.fold_in(splits[21], 71), 0)
    leaf_count = draw_leaf_count(jax.random.fold_in(splits[21], 71), 0)
    mid_src = draw_mid_src(jax.random.fold_in(splits[21], 71), 0)
    mid_count = draw_mid_count(jax.random.fold_in(splits[21], 71), 0)
    box_src = draw_box_src(jax.random.fold_in(splits[21], 71), 0)
    box_count = draw_box_count(jax.random.fold_in(splits[21], 71), 0)
    box_parent = draw_box_parent(jax.random.fold_in(splits[21], 71), 0)
    top_src = with_ends(jax.random.randint(splits[19], (TOP, KF), 0, TOP), jax.random.fold_in(splits[19], 1), 0, TOP - 1).astype(jnp.int32)
    top_count = draw_top_count(jax.random.fold_in(splits[21], 71), 0)
    return {"values": values, "points": points, "basis": basis, "leaf_up": leaf_up, "mid_up": mid_up, "box_up": box_up, "leaf_skel": leaf_skel, "mid_skel": mid_skel, "box_skel": box_skel, "top_skel": top_skel, "near_src": near_src, "near_count": near_count, "leaf_src": leaf_src, "leaf_count": leaf_count, "mid_src": mid_src, "mid_count": mid_count, "box_src": box_src, "box_count": box_count, "box_parent": box_parent, "top_src": top_src, "top_count": top_count}


def kernel_tile(targets, sources):
    first = targets.astype(jnp.float32)
    second = sources.astype(jnp.float32)
    delta_x = first[:, 0, :, None] - second[:, 0, None, :]
    delta_y = first[:, 1, :, None] - second[:, 1, None, :]
    return (0.25 * jnp.exp(-jnp.sqrt(delta_x * delta_x + delta_y * delta_y + 0.0025))).astype(jnp.bfloat16)

def near_sum(values, points, sources, counts, block_size):
    leaves = values.shape[0]

    def one_block(number):
        first_row = (number * block_size).astype(jnp.int32)
        targets = lax.dynamic_slice_in_dim(points, first_row, block_size)
        source_ids = lax.dynamic_slice_in_dim(sources, first_row, block_size)
        live_count = lax.dynamic_slice_in_dim(counts, first_row, block_size)
        running = jnp.zeros((block_size, S, P_SIZE), jnp.float32)
        for column in range(sources.shape[1]):
            picked = source_ids[:, column]
            coupling = kernel_tile(targets, points[picked])
            contrib = jnp.einsum('bsq,bpq->bsp', values[picked].astype(jnp.float32), coupling.astype(jnp.float32))
            running = running + jnp.where((column < live_count)[:, None, None], contrib, 0.0)
        return running
    blocks = lax.map(one_block, jnp.arange(leaves // block_size, dtype=jnp.int32))
    return blocks.reshape(leaves, S, P_SIZE)

def far_sum(coeffs, skeleton, sources, counts, block_size):
    nodes = coeffs.shape[0]
    frames = skeleton.reshape(nodes, 2, R)

    def one_block(number):
        first_row = (number * block_size).astype(jnp.int32)
        targets = lax.dynamic_slice_in_dim(frames, first_row, block_size)
        source_ids = lax.dynamic_slice_in_dim(sources, first_row, block_size)
        live_count = lax.dynamic_slice_in_dim(counts, first_row, block_size)
        running = jnp.zeros((block_size, S, R), jnp.float32)
        for column in range(sources.shape[1]):
            picked = source_ids[:, column]
            coupling = kernel_tile(targets, frames[picked])
            contrib = jnp.einsum('nsq,nrq->nsr', coeffs[picked].astype(jnp.float32), coupling.astype(jnp.float32))
            running = running + jnp.where((column < live_count)[:, None, None], contrib, 0.0)
        return running
    blocks = lax.map(one_block, jnp.arange(nodes // block_size, dtype=jnp.int32))
    return blocks.reshape(nodes, S, R)

def lift_up(coeffs, transfer):
    nodes = coeffs.shape[0]
    matrices = transfer.reshape(nodes, R, R).astype(jnp.float32)
    return jnp.einsum('nsq,nqr->nsr', coeffs.astype(jnp.float32), matrices)

def reference(values, points, basis, leaf_up, mid_up, box_up, leaf_skel, mid_skel, box_skel, top_skel, near_src, near_count, leaf_src, leaf_count, mid_src, mid_count, box_src, box_count, box_parent, top_src, top_count):
    near_field = near_sum(values, points, near_src, near_count, LEAF_DEV)
    leaf_coef = jnp.einsum('tsp,trp->tsr', values.astype(jnp.float32), basis.astype(jnp.float32)).astype(jnp.bfloat16)
    mid_coef = lift_up(leaf_coef, leaf_up).reshape(-1, 4, S, R).sum(axis=1).astype(jnp.bfloat16)
    box_coef = lift_up(mid_coef, mid_up).reshape(-1, 4, S, R).sum(axis=1).astype(jnp.bfloat16)
    box_term = lift_up(box_coef, box_up).astype(jnp.bfloat16)
    top_coef = jax.ops.segment_sum(box_term.astype(jnp.float32), box_parent, num_segments=TOP).astype(jnp.bfloat16)
    leaf_far = far_sum(leaf_coef, leaf_skel, leaf_src, leaf_count, LEAF_DEV)
    mid_far = far_sum(mid_coef, mid_skel, mid_src, mid_count, LEAF_DEV // 4)
    box_far = far_sum(box_coef, box_skel, box_src, box_count, LEAF_DEV // 16)
    top_field = far_sum(top_coef, top_skel, top_src, top_count, TOP).astype(jnp.bfloat16)
    box_field = (box_far + jnp.einsum('bsr,bqr->bsq', top_field[box_parent].astype(jnp.float32), box_up.reshape(-1, R, R).astype(jnp.float32))).astype(jnp.bfloat16)
    mid_field = (mid_far + jnp.einsum('bsr,bjqr->bjsq', box_field.astype(jnp.float32), mid_up.reshape(-1, 4, R, R).astype(jnp.float32)).reshape(-1, S, R)).astype(jnp.bfloat16)
    leaf_field = (leaf_far + jnp.einsum('bsr,bjqr->bjsq', mid_field.astype(jnp.float32), leaf_up.reshape(-1, 4, R, R).astype(jnp.float32)).reshape(-1, S, R)).astype(jnp.bfloat16)
    return near_field + jnp.einsum('tsr,trp->tsp', leaf_field.astype(jnp.float32), basis.astype(jnp.float32))
```

```python
import functools

import jax
import jax.numpy as jnp
from jax import lax
from jax.experimental import pallas as pl
from jax.experimental.pallas import tpu as pltpu
from jax.sharding import PartitionSpec as P

NEG_LOG2E = -1.4426950408889634
EPS = 0.0025


def neighbours(array):
    size = lax.axis_size("leaf")
    up = [(i, (i + 1) % size) for i in range(size - 1)]
    down = [(j, i) for i, j in up]
    return lax.ppermute(array, "leaf", up), lax.ppermute(array, "leaf", down)


def split3(number):
    high = lax.reduce_precision(number, 8, 7)
    rest = number - high
    middle = lax.reduce_precision(rest, 8, 7)
    return [part.astype(jnp.bfloat16) for part in (high, middle, rest - middle)]


def source_rows(x, y):
    wide_x, wide_y = x.astype(jnp.float32), y.astype(jnp.float32)
    ones = jnp.ones_like(x)
    parts = split3(wide_x * wide_x + wide_y * wide_y + EPS)
    return jnp.stack([-2.0 * x, -2.0 * y] + parts + [ones] * 3, axis=1).astype(jnp.bfloat16)


def target_rows(x, y):
    wide_x, wide_y = x.astype(jnp.float32), y.astype(jnp.float32)
    ones = jnp.ones_like(x)
    parts = split3(wide_x * wide_x + wide_y * wide_y)
    rows = jnp.stack([x, y] + [ones] * 3 + parts, axis=1)
    return jnp.pad(rows, ((0, 1), (0, 8), (0, 0)))


def pair_kernel(
    sizes, targets, width, group, stride_bits, unroll, idx, count, frames, *refs
):
    parts = refs[: len(sizes)]
    out, table, items, sems = refs[len(sizes) :]
    copies = []
    start = 0
    for number, size in enumerate(sizes):
        copies.append(
            pltpu.make_async_copy(
                parts[number], table.at[pl.ds(start, size)], sems.at[number]
            )
        )
        start += size
    for copy in copies:
        copy.start()
    table[start] = jnp.zeros(table.shape[1:], table.dtype)
    out[...] = jnp.zeros_like(out)
    most = (items.shape[0] - unroll) // targets

    def enlist(target, position):
        base = lax.shift_left(target, stride_bits)
        for j in range(most):
            items[position + j] = base + group * j
        return position + lax.shift_right_logical(
            count[target] + (group - 1), group.bit_length() - 1
        )

    total = lax.fori_loop(0, targets, enlist, jnp.int32(0))
    for j in range(unroll):
        items[total + j] = jnp.int32(targets << stride_bits)
    for copy in copies:
        copy.wait()
    left = lax.broadcasted_iota(jnp.int32, (16, 128), 1) < 64

    def step(number, carry):
        found = []
        for u in range(unroll):
            code = items[number * unroll + u]
            target = lax.shift_right_logical(code, stride_bits)
            picked = [table[idx[code + j]] for j in range(group)]
            if group == 4:
                picked = [
                    jnp.where(left, picked[0], picked[1]),
                    jnp.where(left, picked[2], picked[3]),
                ]
            record = jnp.concatenate(picked, axis=1)
            frame = frames[target][:, :width]
            square = lax.dot_general(
                frame, record, (((0,), (0,)), ((), ())), preferred_element_type=jnp.float32
            )
            square = jnp.maximum(square, EPS)
            coupling = jnp.exp2(square * lax.rsqrt(square) * NEG_LOG2E).astype(jnp.bfloat16)
            result = lax.dot_general(
                record, coupling, (((1,), (1,)), ((), ())), preferred_element_type=jnp.float32
            )
            found.append((target, 0.25 * result[8:, :]))
        for target, result in found:
            out[target] += result
        return carry

    lax.fori_loop(0, lax.shift_right_logical(total + unroll - 1, unroll.bit_length() - 1), step, 0)


def pair_sum(rows, counts, frames, parts, width, group, unroll):
    targets, slots = rows.shape
    stride_bits = (slots + group - 1).bit_length()
    most = (slots + group - 1) // group
    sizes = tuple(part.shape[0] for part in parts)
    zero_row = sum(sizes)
    idx = jnp.pad(
        rows, ((0, 1), (0, (1 << stride_bits) - slots)), constant_values=zero_row
    ).reshape(-1)
    pairs = targets * slots * 128 * 128
    smem = pl.BlockSpec(memory_space=pltpu.SMEM)
    vmem = pl.BlockSpec(memory_space=pltpu.VMEM)
    return pl.pallas_call(
        functools.partial(
            pair_kernel, sizes, targets, width, group, stride_bits, unroll
        ),
        out_shape=jax.ShapeDtypeStruct((targets + 1, 8, width), jnp.float32),
        in_specs=[smem, smem, vmem] + [pl.BlockSpec(memory_space=pl.ANY)] * len(parts),
        out_specs=vmem,
        scratch_shapes=[
            pltpu.VMEM((zero_row + 1, 16, 128), jnp.bfloat16),
            pltpu.SMEM((targets * most + unroll,), jnp.int32),
            pltpu.SemaphoreType.DMA((len(parts),)),
        ],
        compiler_params=pltpu.CompilerParams(vmem_limit_bytes=40 << 20),
        cost_estimate=pl.CostEstimate(
            flops=pairs * 64, bytes_accessed=zero_row * 4096, transcendentals=pairs * 2
        ),
    )(idx, counts, frames, *parts)


def live_rows(rows, counts, zero_row):
    slots = lax.broadcasted_iota(jnp.int32, rows.shape, 1)
    return jnp.where(slots < counts[:, None], rows, zero_row)


def lift_up(coeffs, transfer, rank_width):
    nodes = coeffs.shape[0]
    matrices = transfer.reshape(nodes, rank_width, rank_width)
    return jnp.einsum("nsq,nqr->nsr", coeffs, matrices, preferred_element_type=jnp.float32)


def twice(array):
    return jnp.concatenate([array, array], axis=-1)


def node_records(coeffs, skeleton, rank_width):
    x, y = skeleton[:, :rank_width], skeleton[:, rank_width:]
    return jnp.concatenate([source_rows(twice(x), twice(y)), twice(coeffs)], axis=1)


def body(
    values,
    points,
    basis,
    leaf_up,
    mid_up,
    box_up,
    leaf_skel,
    mid_skel,
    box_skel,
    top_skel,
    near_src,
    near_count,
    leaf_src,
    leaf_count,
    mid_src,
    mid_count,
    box_src,
    box_count,
    box_parent,
    top_src,
    top_count,
):
    leaves = values.shape[0]
    samples = values.shape[1]
    point_count = values.shape[2]
    rank_width = basis.shape[1]
    middle = leaves // 4
    box_nodes = leaves // 16
    top_nodes = top_count.shape[0]
    device = lax.axis_index("leaf")
    record = jnp.concatenate([source_rows(points[:, 0], points[:, 1]), values], axis=1)
    before, after = neighbours(record)
    top_lists = lax.all_gather(
        jnp.concatenate([top_src, top_count[:, None]], axis=1), "leaf", axis=0, tiled=True
    )
    leaf_coef = jnp.einsum(
        "tsp,trp->tsr", values, basis, preferred_element_type=jnp.float32
    ).astype(jnp.bfloat16)
    mid_coef = (
        lift_up(leaf_coef, leaf_up, rank_width)
        .reshape(middle, 4, samples, rank_width)
        .sum(axis=1)
        .astype(jnp.bfloat16)
    )
    box_coef = (
        lift_up(mid_coef, mid_up, rank_width)
        .reshape(box_nodes, 4, samples, rank_width)
        .sum(axis=1)
        .astype(jnp.bfloat16)
    )
    box_term = (
        lift_up(box_coef, box_up, rank_width)
        .astype(jnp.bfloat16)
        .reshape(box_nodes, samples * rank_width)
    )
    per_device = leaves + middle + box_nodes
    skeletons = jnp.concatenate([leaf_skel, mid_skel, box_skel], axis=0)
    nodes = node_records(
        jnp.concatenate([leaf_coef, mid_coef, box_coef], axis=0), skeletons, rank_width
    )
    nodes_before, nodes_after = neighbours(nodes)
    top_term = (
        box_term.reshape(top_nodes, 4, samples * rank_width)
        .astype(jnp.float32)
        .sum(axis=1)
        .astype(jnp.bfloat16)
    )
    top_coef = lax.all_gather(top_term, "leaf", axis=0, tiled=True)
    order = box_parent.reshape(-1, 4)[:, 0]
    top_count_all = order.shape[0]
    top_records = node_records(
        top_coef.reshape(top_count_all, samples, rank_width), top_skel[order], rank_width
    )
    own_top = lax.dynamic_slice_in_dim(order, device * top_nodes, top_nodes)

    near_rows = live_rows(near_src - (device - 1) * leaves, near_count, 3 * leaves)
    near_field = pair_sum(
        near_rows,
        near_count,
        target_rows(points[:, 0], points[:, 1]),
        (before, record, after),
        point_count,
        2,
        4,
    )[:leaves]

    zero_row = 3 * per_device + top_count_all
    own_lists = top_lists[own_top]
    own_src, own_count = own_lists[:, :-1], own_lists[:, -1]
    place = lax.broadcasted_iota(jnp.int32, (1, 1, top_count_all), 2)
    top_place = jnp.sum(jnp.where(own_src[:, :, None] == order, place, 0), axis=2)

    def table_rows(sources, count, offset):
        held = sources // count
        return (held - device + 1) * per_device + offset + sources - held * count

    far_rows = jnp.concatenate(
        [
            table_rows(leaf_src, leaves, 0),
            table_rows(mid_src, middle, leaves),
            table_rows(box_src, box_nodes, leaves + middle),
            3 * per_device + top_place,
        ],
        axis=0,
    )
    far_count = jnp.concatenate([leaf_count, mid_count, box_count, own_count])
    far_skel = jnp.concatenate([skeletons, top_skel[own_top]], axis=0)
    far = pair_sum(
        live_rows(far_rows, far_count, zero_row),
        far_count,
        target_rows(twice(far_skel[:, :rank_width]), twice(far_skel[:, rank_width:])),
        (nodes_before, nodes, nodes_after, top_records),
        rank_width,
        4,
        4,
    )
    leaf_far = far[:leaves]
    mid_far = far[leaves : leaves + middle]
    box_far = far[leaves + middle : per_device]
    own_field = far[per_device : per_device + top_nodes].astype(jnp.bfloat16)
    parent_field = jnp.repeat(own_field, 4, axis=0)
    box_field = (
        box_far
        + jnp.einsum(
            "bsr,bqr->bsq",
            parent_field,
            box_up.reshape(box_nodes, rank_width, rank_width),
            preferred_element_type=jnp.float32,
        )
    ).astype(jnp.bfloat16)
    mid_down = jnp.einsum(
        "bsr,bjqr->bjsq",
        box_field,
        mid_up.reshape(box_nodes, 4, rank_width, rank_width),
        preferred_element_type=jnp.float32,
    )
    mid_field = (mid_far + mid_down.reshape(middle, samples, rank_width)).astype(jnp.bfloat16)
    leaf_down = jnp.einsum(
        "bsr,bjqr->bjsq",
        mid_field,
        leaf_up.reshape(middle, 4, rank_width, rank_width),
        preferred_element_type=jnp.float32,
    )
    leaf_field = (leaf_far + leaf_down.reshape(leaves, samples, rank_width)).astype(jnp.bfloat16)
    return near_field + jnp.einsum(
        "tsr,trp->tsp", leaf_field, basis, preferred_element_type=jnp.float32
    )


def solution(mesh):
    return jax.shard_map(
        body,
        mesh=mesh,
        in_specs=(
            P("leaf", None, None),
            P("leaf", None, None),
            P("leaf", None, None),
            P("leaf", None),
            P("leaf", None),
            P("leaf", None),
            P("leaf", None),
            P("leaf", None),
            P("leaf", None),
            P(),
            P("leaf", None),
            P("leaf"),
            P("leaf", None),
            P("leaf"),
            P("leaf", None),
            P("leaf"),
            P("leaf", None),
            P("leaf"),
            P(),
            P("leaf", None),
            P("leaf"),
        ),
        out_specs=P("leaf", None, None),
        check_vma=False,
    )
```
